32 devices in a mesh: grp: 2 (over y), gx: 16 (over z, x, core).
Axes of the slice: x: 2, y: 2, z: 4, core: 2. Of those that a mesh axis runs over, the one named last changes fastest.
Arguments:
- state: float32 [5, 192, 16, 128], P(None, ('grp', 'gx')), parts along dimension 1, may hold values from -7.2 to 7.2
- cotangent: float32 [5, 192, 16, 128], P(None, ('grp', 'gx')), parts along dimension 1, may hold values from -6 to 6
- weight_in: float32 [16, 128], replicated, may hold values from -1.5 to 1.5
- bias_in: float32 [128], replicated, may hold values from -3 to 3
- weight_mid: float32 [128, 128], replicated, may hold values from -0.5 to 0.5
- bias_mid: float32 [128], replicated, may hold values from -3 to 3
- weight_out: float32 [128, 6], replicated, may hold values from -0.5 to 0.5
- cell_index: int32 [2, 1024], P(None, 'grp'), parts along dimension 1, may hold values from 0 to 196607
- segment_id: int32 [2, 1024], P(None, 'grp'), parts along dimension 1, may hold values from 0 to 63
- segment_coef: float32 [64], replicated, may hold values from 0.1 to 1
Outputs:
- grad_state: float32 [5, 192, 16, 128], P(None, ('grp', 'gx')), parts along dimension 1
- grad_weight_in: float32 [32, 128], P('grp'), parts along dimension 0
- grad_bias_in: float32 [256], P('grp'), parts along dimension 0
- grad_weight_mid: float32 [256, 128], P('grp'), parts along dimension 0
- grad_bias_mid: float32 [256], P('grp'), parts along dimension 0
- grad_weight_out: float32 [256, 6], P('grp'), parts along dimension 0
The draws below stay inside these ranges and needn't reach their ends.
There are 2 independent parts, one for each index of `grp`. The reference program is written for one: setup_inputs(seed, part) draws one part's arguments, and reference() takes and returns one part's arrays. A program takes and returns all parts, laid end to end along the dimension named above; an argument that names none is the same for every part. Nothing has to cross between parts.
Inputs may be any that keep to these rules, and one draw needn't show every extreme that they name: `cell_index`: flat cell indices; a cell may appear more than once.
All inputs are finite; a program needn't handle non-finite values.
Results may differ from the reference program's by a relative error of at most 0.000098.
Values sent between devices are 32-bit elements; how exact they have to be, the bound alone decides.
A program may use at most 64 MiB of HBM per device.

```python
import math
import jax
import jax.numpy as jnp
from jax import lax

NY = 16
NZ = 128
FEAT = 16
HID = 128
OUTS = 6
SEGS = 64
NX = 96
NACT = 512


def draw_state(key, part):
    key = jax.random.fold_in(key, 11)
    position = jnp.arange(NX, dtype=jnp.float32) / NX
    raw = jnp.clip(jax.random.normal(key, (5, NX, NY, NZ), jnp.float32), -4.0, 4.0)
    ramp = 0.6 + 1.2 * position
    return raw * ramp[None, :, None, None]


def with_ends(values, key, low, high):
    extent = values.shape
    index_at = [jax.random.randint(jax.random.fold_in(key, axis), (), 0, extent[axis]) for axis in range(len(extent))]
    values = values.at[tuple(index_at)].set(low)
    longest = extent.index(max(extent))
    index_at[longest] = (index_at[longest] + 1) % extent[longest]
    return values.at[tuple(index_at)].set(high)


def block_scale(key, shape, cuts, low, top_value):
    gain, own = 1.0, jax.random.fold_in(key, 6)
    for dim, shards_of in cuts:
        steps = jnp.exp(jax.random.uniform(jax.random.fold_in(own, dim), (shards_of,), jnp.float32, low / len(cuts), top_value / len(cuts)))
        gain = gain * jnp.repeat(steps, shape[dim] // shards_of).reshape([-1 if axis == dim else 1 for axis in range(len(shape))])
    return gain


def noise(key, extent, deviation, bound, shards=(), kind=jnp.bfloat16):
    array = jax.random.normal(key, extent, jnp.float32) * deviation
    if len(shards) > 0:
        array = block_scale(key, extent, shards, -0.22, 0.18) * array
    return jnp.clip(array, min=-bound, max=bound).astype(kind)


def setup_inputs(seed: int = 0, part: int = 0) -> dict:
    streams_of = jax.random.split(jax.random.key(seed), 11)
    part_splits = jax.random.split(jax.random.fold_in(streams_of[10], part), 11)
    state = draw_state(jax.random.fold_in(jax.random.fold_in(streams_of[10], part), 71), part)
    cotangent = noise(part_splits[1], (5, NX, NY, NZ), 1.0, 6.0, ((1, 16),), jnp.float32)
    weight_in = noise(streams_of[2], (FEAT, HID), FEAT ** -0.5, 1.5, (), jnp.float32)
    bias_in = noise(streams_of[3], (HID,), 0.5, 3.0, (), jnp.float32)
    weight_mid = noise(streams_of[4], (HID, HID), HID ** -0.5, 0.5, (), jnp.float32)
    bias_mid = noise(streams_of[5], (HID,), 0.5, 3.0, (), jnp.float32)
    weight_out = noise(streams_of[6], (HID, OUTS), HID ** -0.5, 0.5, (), jnp.float32)
    cell_index = with_ends(jax.random.randint(part_splits[7], (2, NACT), 0, NX * NY * NZ), jax.random.fold_in(part_splits[7], 1), 0, (NX * NY * NZ) - 1).astype(jnp.int32)
    segment_id = with_ends(jax.random.randint(part_splits[8], (2, NACT), 0, SEGS), jax.random.fold_in(part_splits[8], 1), 0, SEGS - 1).astype(jnp.int32)
    segment_coef = jnp.clip(jnp.exp(jax.random.uniform(streams_of[9], (SEGS,), jnp.float32, math.log(0.1), math.log(1.0))), 0.1, 1.0)
    return {"state": state, "cotangent": cotangent, "weight_in": weight_in, "bias_in": bias_in, "weight_mid": weight_mid, "bias_mid": bias_mid, "weight_out": weight_out, "cell_index": cell_index, "segment_id": segment_id, "segment_coef": segment_coef}


MEAN_WIND = 0.5
TIME_STEP = 0.2
CLOSURE_SCALE = 0.1
EPSILON = 1e-05
HIGHEST_PRECISION = lax.Precision.HIGHEST

def along_x(source, low_plane, high_plane):
    return (source[:, low_plane + 1:high_plane + 1] - source[:, low_plane - 1:high_plane - 1]) * 0.5

def along_y(source):
    return (jnp.roll(source, -1, axis=-2) - jnp.roll(source, 1, axis=-2)) * 0.5

def along_z(source):
    return (jnp.roll(source, -1, axis=-1) - jnp.roll(source, 1, axis=-1)) * 0.5

def velocity_gradient(padded, low_plane, high_plane):
    velocity = padded[1:4]
    centre = velocity[:, low_plane:high_plane]
    return jnp.stack([along_x(velocity, low_plane, high_plane), along_y(centre), along_z(centre)], axis=1)

def square_sum(padded, low_plane, high_plane):
    gradient = velocity_gradient(padded, low_plane, high_plane)
    return jnp.sum(gradient * gradient)

def closure_block(feature, weights):
    weight_in, bias_in, weight_mid, bias_mid, weight_out = weights
    hidden_one = jnp.tanh(jnp.dot(weight_in.T, feature, precision=HIGHEST_PRECISION, preferred_element_type=jnp.float32) + bias_in[:, None])
    hidden_two = jnp.tanh(jnp.dot(weight_mid.T, hidden_one, precision=HIGHEST_PRECISION, preferred_element_type=jnp.float32) + bias_mid[:, None])
    return CLOSURE_SCALE * jnp.dot(weight_out.T, hidden_two, precision=HIGHEST_PRECISION, preferred_element_type=jnp.float32)

def subgrid_stress(padded, scale, weights):
    planes = padded.shape[1]
    span_y = padded.shape[2]
    span_z = padded.shape[3]
    count = planes - 4
    gradient = velocity_gradient(padded, 2, planes - 2) / scale
    strain = 0.5 * (gradient + jnp.swapaxes(gradient, 0, 1))
    spin = 0.5 * (gradient - jnp.swapaxes(gradient, 0, 1))
    centre = padded[:, 2:planes - 2]
    stacked = jnp.concatenate([gradient.reshape(9, count, span_y, span_z), centre[1:4], centre[0:1], centre[4:5], lax.optimization_barrier(jnp.sum(strain * strain, axis=(0, 1)))[None], lax.optimization_barrier(jnp.sum(spin * spin, axis=(0, 1)))[None]], axis=0)
    feature = jnp.transpose(stacked.reshape(16, count, span_y * span_z), (1, 0, 2))
    saved = jax.checkpoint(closure_block)
    stress = lax.map(lambda block: saved(block, weights), feature)
    return jnp.transpose(stress, (1, 0, 2)).reshape(6, count, span_y, span_z)

def forcing(velocity_x, cell_index, segment_id, segment_coef, start, total):
    count = velocity_x.shape[0]
    plane_cells = velocity_x.shape[1] * velocity_x.shape[2]
    plane = cell_index // plane_cells
    local = (plane - start) % total
    inside = local < count
    flat = jnp.where(inside, local * plane_cells + cell_index % plane_cells, count * plane_cells).astype(jnp.int32)
    speed = MEAN_WIND + jnp.take(velocity_x.reshape(-1), flat, mode='clip')
    selector = (segment_id[:, None] == jnp.arange(segment_coef.shape[0], dtype=jnp.int32)[None, :]).astype(jnp.float32)
    coefficient = jnp.dot(selector, segment_coef, precision=HIGHEST_PRECISION, preferred_element_type=jnp.float32)
    thrust = -coefficient * speed * jnp.abs(speed)
    empty = jnp.zeros((count * plane_cells,), jnp.float32)
    return empty.at[flat].add(thrust, mode='drop').reshape(velocity_x.shape)

def tendency(padded, scale, weights, cell_index, segment_id, segment_coef, start, total):
    planes = padded.shape[1]
    stress = subgrid_stress(padded, scale, weights)
    middle = stress[:, 1:-1]

    def stress_x(entry):
        return (stress[entry, 2:] - stress[entry, :-2]) * 0.5
    subgrid_x = stress_x(0) + along_y(middle[3]) + along_z(middle[4])
    subgrid_y = stress_x(3) + along_y(middle[1]) + along_z(middle[5])
    subgrid_z = stress_x(4) + along_y(middle[5]) + along_z(middle[2])
    centre = padded[:, 3:planes - 3]
    upwind = (2.0 * padded[:, 4:planes - 2] + 3.0 * centre - 6.0 * padded[:, 2:planes - 4] + padded[:, 1:planes - 5]) / 6.0
    pressure_x = along_x(padded[4:5], 3, planes - 3)[0]
    divergence = along_x(padded[1:2], 3, planes - 3)[0] + along_y(centre[2]) + along_z(centre[3])
    thrust = forcing(centre[1], cell_index, segment_id, segment_coef, start, total)
    advect = -MEAN_WIND * upwind
    return jnp.stack([advect[0] - divergence, advect[1] - pressure_x + subgrid_x + thrust, advect[2] - along_y(centre[4]) + subgrid_y, advect[3] - along_z(centre[4]) + subgrid_z, advect[4] - divergence], axis=0)

def periodic(current, depth):
    return jnp.concatenate([current[:, -depth:], current, current[:, :depth]], axis=1)

def reference(state, cotangent, weight_in, bias_in, weight_mid, bias_mid, weight_out, cell_index, segment_id, segment_coef):
    total = state.shape[1]
    cells = state.shape[1] * state.shape[2] * state.shape[3]

    def section(current, weights, slot):
        padded = periodic(current, 3)
        scale = lax.stop_gradient(jnp.sqrt(square_sum(padded, 3, total + 3) / cells + EPSILON))
        return tendency(padded, scale, weights, cell_index[slot], segment_id[slot], segment_coef, 0, total)

    def forward(initial, weights):
        middle = initial + TIME_STEP * section(initial, weights, 0)
        return 0.75 * initial + 0.25 * (middle + TIME_STEP * section(middle, weights, 1))
    weights = (weight_in, bias_in, weight_mid, bias_mid, weight_out)
    _, pullback = jax.vjp(forward, state, weights)
    grad_state, grads = pullback(cotangent)
    factor = 1.0 / (TIME_STEP * CLOSURE_SCALE * math.sqrt(cells))
    return (grad_state, grads[0] * factor, grads[1] * factor, grads[2] * factor, grads[3] * factor, grads[4] * factor)
```

```python
import functools
import math

import jax
import jax.numpy as jnp
from jax import lax
from jax.experimental import pallas as pl
from jax.experimental.pallas import tpu as pltpu
from jax.sharding import PartitionSpec as P

MEAN_WIND = 0.5
TIME_STEP = 0.2
CLOSURE_SCALE = 0.1
EPSILON = 1e-05
F32 = jnp.float32
BF16 = jnp.bfloat16
ROWS = 8
GROUP = 16
MESH = pl.DeviceIdType.MESH


def split(value):
    high = value.astype(BF16)
    return high, (value - high.astype(F32)).astype(BF16)


def dot(left, right):
    return jnp.dot(left, right, preferred_element_type=F32)


def dot_nt(left, right):
    return lax.dot_general(left, right, (((1,), (1,)), ((), ())), preferred_element_type=F32)


def along_y(field):
    return (pltpu.roll(field, field.shape[1] - 1, 1) - pltpu.roll(field, 1, 1)) * 0.5


def along_z(field):
    return (pltpu.roll(field, field.shape[2] - 1, 2) - pltpu.roll(field, 1, 2)) * 0.5


def kernel(
    count,
    cells,
    state,
    cotangent,
    weight_in,
    bias_in,
    weight_mid,
    bias_mid,
    weight_out,
    cell_index,
    segment_id,
    segment_coef,
    grad_state,
    grad_in,
    grad_bias_in,
    grad_mid,
    grad_bias_mid,
    grad_out,
    pad_state,
    pad_middle,
    pad_cot,
    pad_carry,
    pad_stress,
    pad_grad,
    send_stress,
    send_grad,
    feats,
    stress,
    dstress,
    dfeats,
    hidden_one,
    hidden_two,
    left_one,
    left_mid,
    left_stress,
    left_out,
    left_back,
    left_feat,
    bias_two,
    acc_mid,
    acc_in,
    acc_out,
    sum_slots,
    sum_far,
    grad_parts,
    grad_slots,
    grad_total,
    grad_far,
    halo_send,
    halo_recv,
    sum_send,
    sum_recv,
    red_send,
    red_recv,
    gat_send,
    gat_recv,
    far_send,
    far_recv,
):
    planes = state.shape[1]
    span = state.shape[2]
    lanes = state.shape[3]
    rows = planes * span
    wide = ROWS * lanes
    per_plane = span // ROWS
    hid = weight_mid.shape[0]
    far = count // GROUP
    me = lax.axis_index("gx")
    mine = lax.rem(me, GROUP)
    base = me - mine
    block = me // GROUP
    right = lax.rem(me + 1, count)
    left = lax.rem(me + count - 1, count)

    def mate(step):
        return lax.rem(mine + step, GROUP)

    def far_mate(step):
        return lax.rem(block + step, far)

    barrier = pltpu.get_barrier_semaphore()
    for peer in (left, right):
        pl.semaphore_signal(barrier, inc=1, device_id={"gx": peer}, device_id_type=MESH)
    for step in range(1, GROUP):
        pl.semaphore_signal(barrier, inc=1, device_id={"gx": base + mate(step)}, device_id_type=MESH)
    for step in range(1, far):
        pl.semaphore_signal(
            barrier, inc=1, device_id={"gx": far_mate(step) * GROUP + mine}, device_id_type=MESH
        )
    pl.semaphore_wait(barrier, 2 + GROUP - 1 + far - 1)

    def remote(source, target, send, recv, peer):
        copy = pltpu.make_async_remote_copy(
            src_ref=source,
            dst_ref=target,
            send_sem=send,
            recv_sem=recv,
            device_id={"gx": peer},
            device_id_type=MESH,
        )
        copy.start()
        return copy

    def exchange(slot, to_right, at_low, to_left, at_high):
        return (
            remote(to_right, at_low, halo_send.at[slot, 0], halo_recv.at[slot, 0], right),
            remote(to_left, at_high, halo_send.at[slot, 1], halo_recv.at[slot, 1], left),
        )

    def finish(copies):
        for copy in copies:
            copy.wait()

    def halo(slot, source, start, target, low, high):
        return exchange(
            slot,
            source.at[:, start + planes - low : start + planes],
            target.at[:, 0:low],
            source.at[:, start : start + high],
            target.at[:, low + planes : low + planes + high],
        )

    state_copies = halo(0, state, 0, pad_state, 2, 1)
    cot_copies = halo(1, cotangent, 0, pad_cot, 1, 2)
    pad_state[:, 2 : 2 + planes] = state[...]
    pad_cot[:, 1 : 1 + planes] = cotangent[...]

    zeros_tail = jnp.zeros((8, lanes), F32)
    pack = jnp.concatenate(
        [weight_in[...], bias_in[...], bias_mid[...], weight_out[...], zeros_tail], axis=0
    )
    pack_high, pack_low = split(pack)
    high = pack_high.astype(F32)
    low = pack_low.astype(F32)

    def turned(parts):
        used = sum(part.shape[0] for part in parts)
        return jnp.concatenate(parts + [jnp.zeros((hid - used, lanes), F32)], axis=0).T.astype(BF16)

    left_one[...] = turned([high[:16], high[:16], low[:16], high[16:], low[16:]])
    left_stress[...] = turned([high[16:], high[16:], low[16:]])

    def stacked(value_high, value_low):
        return jnp.concatenate(
            [
                jnp.concatenate([value_high, value_high], axis=1),
                jnp.concatenate([value_low, value_low], axis=1),
            ],
            axis=0,
        )

    left_mid[...] = stacked(*split(weight_mid[...].T))
    left_back[...] = stacked(*split(weight_mid[...]))
    left_out[...] = stacked(pack_high[16:], pack_low[16:])
    left_feat[...] = stacked(pack_high[:16], pack_low[:16])
    turned_bias = jnp.concatenate([bias_mid[...], jnp.zeros((hid - 1, lanes), F32)], axis=0).T
    bias_two[...] = jnp.broadcast_to(turned_bias[:, 0:1], (hid, lanes))
    first_row = lax.broadcasted_iota(jnp.int32, (16, wide), 0) == 0
    ones_row = jnp.where(first_row, 1.0, 0.0).astype(BF16)

    def cell_coefficient(slot):
        index = cell_index[slot : slot + 1, :]
        points = index.shape[1]
        segments = segment_coef.shape[1]
        chosen = (
            lax.broadcasted_iota(jnp.int32, (segments, points), 0) == segment_id[slot : slot + 1, :]
        )
        picked = jnp.where(chosen, 1.0, 0.0)
        coef = lax.dot(
            jnp.broadcast_to(segment_coef[...], (8, segments)),
            picked,
            precision=lax.Precision.HIGHEST,
            preferred_element_type=F32,
        )[0:1]
        row = lax.div(index, jnp.int32(lanes)) - me * rows
        lane = lax.rem(index, jnp.int32(lanes))
        at_row = jnp.where(lax.broadcasted_iota(jnp.int32, (rows, points), 0) == row, 1.0, 0.0)
        at_lane = jnp.where(lax.broadcasted_iota(jnp.int32, (lanes, points), 0) == lane, coef, 0.0)
        return lax.dot_general(
            at_row,
            at_lane,
            (((1,), (1,)), ((), ())),
            precision=lax.Precision.HIGHEST,
            preferred_element_type=F32,
        ).reshape(planes, span, lanes)

    coef_zero = cell_coefficient(0)
    coef_one = cell_coefficient(1)
    acc_mid[...] = jnp.zeros_like(acc_mid)
    acc_in[...] = jnp.zeros_like(acc_in)
    acc_out[...] = jnp.zeros_like(acc_out)
    dstress[...] = jnp.zeros_like(dstress)

    def shifted(ref, comp, low, shift):
        return ref[comp, low + shift : low + shift + planes]

    def along_x(ref, comp, low):
        return (shifted(ref, comp, low, 1) - shifted(ref, comp, low, -1)) * 0.5

    def gradients(ref):
        table = []
        for comp in (1, 2, 3):
            centre = shifted(ref, comp, 2, 0)
            table.append([along_x(ref, comp, 2), along_y(centre), along_z(centre)])
        return table

    def scale_start(slot, table):
        total = None
        for line in table:
            for entry in line:
                total = entry * entry if total is None else total + entry * entry
        total = jnp.sum(total, axis=0)
        total = jnp.sum(total, axis=0, keepdims=True)
        sum_slots[slot, mine] = total
        return [
            remote(
                sum_slots.at[slot, mine],
                sum_slots.at[slot, mine],
                sum_send.at[slot, step],
                sum_recv.at[slot, step],
                base + mate(step),
            )
            for step in range(1, GROUP)
        ]

    def wait_sums(slot, copies):
        for step, copy in zip(range(1, GROUP), copies):
            copy.wait_send()
            source = mate(GROUP - step)
            pltpu.make_async_remote_copy(
                src_ref=sum_slots.at[slot, source],
                dst_ref=sum_slots.at[slot, source],
                send_sem=sum_send.at[slot, step],
                recv_sem=sum_recv.at[slot, step],
                device_id={"gx": base + mate(step)},
                device_id_type=MESH,
            ).wait_recv()

    def scale_finish(slot, copies):
        wait_sums(slot, copies)
        total = jnp.sum(sum_slots[slot], axis=0)
        if far > 1:
            sum_far[slot, 0] = total
            others = [
                remote(
                    sum_far.at[slot, 0],
                    sum_far.at[slot, step],
                    far_send.at[slot, step],
                    far_recv.at[slot, step],
                    far_mate(step) * GROUP + mine,
                )
                for step in range(1, far)
            ]
            finish(others)
            total = jnp.sum(sum_far[slot], axis=0)
        total = jnp.sum(total, axis=1, keepdims=True)
        return lax.rsqrt(total / cells + EPSILON).reshape(1, 1, 1)

    def put(ref, slot, width, value):
        ref[pl.ds(slot, rows, stride=width), :] = value.reshape(rows, lanes)

    def get(ref, slot, width, plane=0, number=planes):
        start = plane * span * width + slot
        return ref[pl.ds(start, number * span, stride=width), :].reshape(number, span, lanes)

    def write_features(section, ref, table, inverse):
        target = feats.at[section]
        scaled = [[entry * inverse for entry in line] for line in table]
        sym = None
        skew = None
        for a in range(3):
            for b in range(3):
                put(target, 3 * a + b, 16, scaled[a][b])
                plus = 0.5 * (scaled[a][b] + scaled[b][a])
                minus = 0.5 * (scaled[a][b] - scaled[b][a])
                sym = plus * plus if sym is None else sym + plus * plus
                if a != b:
                    skew = minus * minus if skew is None else skew + minus * minus
        for slot, comp in enumerate((1, 2, 3, 0, 4)):
            put(target, 9 + slot, 16, shifted(ref, comp, 2, 0))
        put(target, 14, 16, sym)
        put(target, 15, 16, skew)

    def columns(ref, chunk, height):
        start = chunk * (ROWS * height)
        return jnp.concatenate(
            [
                ref[pl.ds(pl.multiple_of(start + row * height, 8), height), :]
                for row in range(ROWS)
            ],
            axis=1,
        )

    def spread(ref, chunk, height, value):
        start = chunk * (ROWS * height)
        for row in range(ROWS):
            ref[pl.ds(pl.multiple_of(start + row * height, 8), height), :] = value[
                :height, row * lanes : (row + 1) * lanes
            ]

    def halves(value):
        size = value.shape[0] // 2
        return value[:size] + value[size:]

    def forward(section, chunk):
        feat_high, feat_low = split(columns(feats.at[section], chunk, 16))
        blank = jnp.zeros((hid - 80, wide), BF16)
        one = jnp.tanh(
            dot(
                left_one[...],
                jnp.concatenate([feat_high, feat_low, feat_high, ones_row, ones_row, blank], axis=0),
            )
        )
        one_parts = jnp.concatenate(split(one), axis=0)
        bias = jnp.concatenate([bias_two[...]] * ROWS, axis=1)
        two = jnp.tanh(halves(dot(left_mid[...], one_parts)) + bias)
        two_parts = jnp.concatenate(split(two), axis=0)
        return (feat_high, feat_low), one, one_parts, two, two_parts

    def backward(chunk, feat, one, one_parts, two, two_parts):
        small = jnp.concatenate([columns(dstress, chunk, 8), jnp.zeros((8, wide), F32)], axis=0)
        small_high, small_low = split(small)
        blank = jnp.zeros((hid - 48, wide), BF16)
        back_two = dot(
            left_stress[...],
            jnp.concatenate([small_high, small_low, small_high, blank], axis=0),
        )
        pre_two = jnp.concatenate(split(back_two * (1.0 - two * two)), axis=0)
        back_one = halves(dot(left_back[...], pre_two))
        pre_one = jnp.concatenate(split(back_one * (1.0 - one * one)), axis=0)
        spread(dfeats, chunk, 16, halves(dot(left_feat[...], pre_one)))
        acc_mid[...] += dot_nt(jnp.concatenate([one_parts, ones_row], axis=0), pre_two)
        acc_in[...] += dot_nt(jnp.concatenate([feat[0], feat[1], ones_row], axis=0), pre_one)
        acc_out[...] += dot_nt(jnp.concatenate([small_high, small_low], axis=0), two_parts)

    def forward_zero(chunk):
        _, one, _, two, two_parts = forward(0, chunk)
        hidden_one[chunk] = one
        hidden_two[chunk] = two
        spread(stress, chunk, 8, halves(dot(left_out[...], two_parts)))

    def both_one(chunk):
        backward(chunk, *forward(1, chunk))

    def backward_zero(chunk):
        one = hidden_one[chunk]
        two = hidden_two[chunk]
        feat = split(columns(feats.at[0], chunk, 16))
        one_parts = jnp.concatenate(split(one), axis=0)
        two_parts = jnp.concatenate(split(two), axis=0)
        backward(chunk, feat, one, one_parts, two, two_parts)

    def sweep(body, between):
        edge = 2 * per_plane

        def outer(step, carry):
            body(jnp.where(step < per_plane, step, step + (planes - 2) * per_plane))
            return carry

        def inner(step, carry):
            body(step)
            return carry

        lax.fori_loop(0, edge, outer, 0)
        between()
        lax.fori_loop(per_plane, (planes - 1) * per_plane, inner, 0)

    def upwind(ref, comp):
        return (
            2.0 * shifted(ref, comp, 2, 1)
            + 3.0 * shifted(ref, comp, 2, 0)
            - 6.0 * shifted(ref, comp, 2, -1)
            + shifted(ref, comp, 2, -2)
        ) * (-MEAN_WIND / 6.0)

    def upwind_back(ref, comp):
        return (
            2.0 * shifted(ref, comp, 1, -1)
            + 3.0 * shifted(ref, comp, 1, 0)
            - 6.0 * shifted(ref, comp, 1, 1)
            + shifted(ref, comp, 1, 2)
        ) * (-MEAN_WIND / 6.0)

    def write_dstress(ref, factor):
        factor = -factor * CLOSURE_SCALE
        u, v, w = (shifted(ref, comp, 1, 0) for comp in (1, 2, 3))
        put(dstress, 2, 8, along_x(ref, 1, 1) * factor)
        put(dstress, 3, 8, along_y(v) * factor)
        put(dstress, 4, 8, along_z(w) * factor)
        put(dstress, 5, 8, (along_y(u) + along_x(ref, 2, 1)) * factor)
        put(dstress, 6, 8, (along_z(u) + along_x(ref, 3, 1)) * factor)
        put(dstress, 7, 8, (along_z(v) + along_y(w)) * factor)

    def dgradient(section, a, b, inverse, plane, number):
        ref = feats.at[section]
        total = get(dfeats, 3 * a + b, 16, plane, number)
        sym = get(dfeats, 14, 16, plane, number)
        here = get(ref, 3 * a + b, 16, plane, number)
        there = get(ref, 3 * b + a, 16, plane, number)
        total = total + (here + there) * sym
        if a != b:
            total = total + (here - there) * get(dfeats, 15, 16, plane, number)
        return total * inverse

    def send_dgradient(section, inverse):
        for a in range(3):
            send_grad[section, 0, a] = dgradient(section, a, 0, inverse, planes - 1, 1)
            send_grad[section, 1, a] = dgradient(section, a, 0, inverse, 0, 1)
        return exchange(
            5 + section,
            send_grad.at[section, 0],
            pad_grad.at[section, :, 0:1],
            send_grad.at[section, 1],
            pad_grad.at[section, :, planes + 1 : planes + 2],
        )

    def back_linear(ref, factor, speed_ref, coef):
        mass_rho = shifted(ref, 0, 1, 0) + shifted(ref, 4, 1, 0)
        mass_x = along_x(ref, 0, 1) + along_x(ref, 4, 1)
        u, v, w = (shifted(ref, comp, 1, 0) for comp in (1, 2, 3))
        speed = MEAN_WIND + shifted(speed_ref, 1, 2, 0)
        return [
            upwind_back(ref, 0) * factor,
            (upwind_back(ref, 1) + mass_x - 2.0 * coef * jnp.abs(speed) * u) * factor,
            (upwind_back(ref, 2) + along_y(mass_rho)) * factor,
            (upwind_back(ref, 3) + along_z(mass_rho)) * factor,
            (upwind_back(ref, 4) + along_x(ref, 1, 1) + along_y(v) + along_z(w)) * factor,
        ]

    def back_closure(section, inverse, linear, copies):
        for a in range(3):
            pad_grad[section, a, 1 : 1 + planes] = dgradient(section, a, 0, inverse, 0, planes)
        total = list(linear)
        for slot, comp in enumerate((1, 2, 3, 0, 4)):
            total[comp] = total[comp] + get(dfeats, 9 + slot, 16)
        for a in range(3):
            total[1 + a] = (
                total[1 + a]
                - along_y(dgradient(section, a, 1, inverse, 0, planes))
                - along_z(dgradient(section, a, 2, inverse, 0, planes))
            )
        finish(copies)
        ref = pad_grad.at[section]
        for a in range(3):
            total[1 + a] = total[1 + a] - along_x(ref, a, 1)
        return total

    finish(state_copies)
    table = gradients(pad_state)
    copies = scale_start(0, table)
    divergence = table[0][0] + table[1][1] + table[2][2]
    speed = MEAN_WIND + shifted(pad_state, 1, 2, 0)
    pressure = shifted(pad_state, 4, 2, 0)
    rate = [
        upwind(pad_state, 0) - divergence,
        upwind(pad_state, 1) - along_x(pad_state, 4, 2) - coef_zero * speed * jnp.abs(speed),
        upwind(pad_state, 2) - along_y(pressure),
        upwind(pad_state, 3) - along_z(pressure),
        upwind(pad_state, 4) - divergence,
    ]
    for comp in range(5):
        pad_middle[comp, 2 : 2 + planes] = (
            shifted(pad_state, comp, 2, 0) + TIME_STEP * rate[comp]
        )
    finish(cot_copies)
    write_dstress(pad_cot, 0.25 * TIME_STEP)
    inverse_zero = scale_finish(0, copies)
    write_features(0, pad_state, table, inverse_zero)
    stress_copies = []

    def send_edges():
        for slot, entry in enumerate((0, 3, 4)):
            send_stress[0, slot] = get(stress, 2 + entry, 8, planes - 1, 1)
            send_stress[1, slot] = get(stress, 2 + entry, 8, 0, 1)
        stress_copies.extend(
            exchange(
                2,
                send_stress.at[0],
                pad_stress.at[:, 0:1],
                send_stress.at[1],
                pad_stress.at[:, planes + 1 : planes + 2],
            )
        )

    sweep(forward_zero, send_edges)
    for slot, entry in enumerate((0, 3, 4)):
        pad_stress[slot, 1 : 1 + planes] = get(stress, 2 + entry, 8)
    s_yy, s_zz, s_xy, s_xz, s_yz = (get(stress, 2 + entry, 8) for entry in (1, 2, 3, 4, 5))
    sub_x = along_y(s_xy) + along_z(s_xz)
    sub_y = along_y(s_yy) + along_z(s_yz)
    sub_z = along_y(s_yz) + along_z(s_zz)
    finish(stress_copies)
    gain = TIME_STEP * CLOSURE_SCALE
    for slot, sub in enumerate((sub_x, sub_y, sub_z)):
        here = shifted(pad_middle, 1 + slot, 2, 0)
        pad_middle[1 + slot, 2 : 2 + planes] = here + gain * (sub + along_x(pad_stress, slot, 1))

    finish(halo(3, pad_middle, 2, pad_middle, 2, 1))
    table = gradients(pad_middle)
    copies = scale_start(1, table)
    linear = back_linear(pad_cot, 0.25 * TIME_STEP, pad_middle, coef_one)
    for comp in range(5):
        linear[comp] = linear[comp] + 0.25 * cotangent[comp]
    inverse_one = scale_finish(1, copies)
    write_features(1, pad_middle, table, inverse_one)
    grad_copies = []
    sweep(both_one, lambda: grad_copies.extend(send_dgradient(1, inverse_one)))
    carried = back_closure(1, inverse_one, linear, grad_copies)
    for comp in range(5):
        pad_carry[comp, 1 : 1 + planes] = carried[comp]

    finish(halo(4, pad_carry, 1, pad_carry, 1, 2))
    write_dstress(pad_carry, TIME_STEP)
    linear = back_linear(pad_carry, TIME_STEP, pad_state, coef_zero)
    for comp in range(5):
        linear[comp] = linear[comp] + (0.75 * cotangent[comp] + shifted(pad_carry, comp, 1, 0))
    grad_copies = []
    sweep(backward_zero, lambda: grad_copies.extend(send_dgradient(0, inverse_zero)))

    factor = 1.0 / (TIME_STEP * CLOSURE_SCALE * math.sqrt(cells))

    def folded(value):
        return (value[:, :hid] + value[:, hid:]) * factor

    both = folded(acc_mid[...])
    mid = both[:hid] + both[hid : 2 * hid]
    narrow = folded(acc_in[...])
    out = folded(acc_out[...])
    rest = jnp.concatenate(
        [
            narrow[:16] + narrow[16:32],
            narrow[32:33],
            both[2 * hid : 2 * hid + 1],
            (out[:16] + out[16:])[2:8],
        ],
        axis=0,
    )
    for slot in range(GROUP):
        grad_parts[slot, 0:8] = mid[8 * slot : 8 * slot + 8]
        if slot < 3:
            grad_parts[slot, 8:16] = rest[8 * slot : 8 * slot + 8]
        else:
            grad_parts[slot, 8:16] = jnp.zeros((8, lanes), F32)
    reduce_copies = [
        remote(
            grad_parts.at[mate(step)],
            grad_slots.at[step],
            red_send.at[step],
            red_recv.at[step],
            base + mate(step),
        )
        for step in range(1, GROUP)
    ]
    result = back_closure(0, inverse_zero, linear, grad_copies)
    for comp in range(5):
        grad_state[comp] = result[comp]
    grad_slots[0] = grad_parts[mine]
    finish(reduce_copies)
    owned = jnp.sum(grad_slots[...], axis=0)
    if far > 1:
        grad_far[0] = owned
        others = [
            remote(
                grad_far.at[0],
                grad_far.at[step],
                far_send.at[2, step],
                far_recv.at[2, step],
                far_mate(step) * GROUP + mine,
            )
            for step in range(1, far)
        ]
        finish(others)
        owned = jnp.sum(grad_far[...], axis=0)
    grad_total[mine] = owned
    gather_copies = [
        remote(
            grad_total.at[mine],
            grad_total.at[mine],
            gat_send.at[step],
            gat_recv.at[step],
            base + mate(step),
        )
        for step in range(1, GROUP)
    ]
    for step, copy in zip(range(1, GROUP), gather_copies):
        copy.wait_send()
        source = mate(GROUP - step)
        pltpu.make_async_remote_copy(
            src_ref=grad_total.at[source],
            dst_ref=grad_total.at[source],
            send_sem=gat_send.at[step],
            recv_sem=gat_recv.at[step],
            device_id={"gx": base + mate(step)},
            device_id_type=MESH,
        ).wait_recv()
    for slot in range(GROUP):
        grad_mid[8 * slot : 8 * slot + 8, :] = grad_total[slot, 0:8]
    grad_in[0:8, :] = grad_total[0, 8:16]
    grad_in[8:16, :] = grad_total[1, 8:16]
    grad_bias_in[...] = grad_total[2, 8:9]
    grad_bias_mid[...] = grad_total[2, 9:10]
    grad_out[...] = grad_total[2, 10:16]


def shards(
    state,
    cotangent,
    weight_in,
    bias_in,
    weight_mid,
    bias_mid,
    weight_out,
    cell_index,
    segment_id,
    segment_coef,
):
    count = lax.axis_size("gx")
    planes, span, lanes = state.shape[1:]
    cells = count * planes * span * lanes
    rows = planes * span
    chunks = rows // ROWS
    wide = ROWS * lanes
    hid = weight_mid.shape[0]
    far = count // GROUP
    dma = pltpu.SemaphoreType.DMA
    vmem = pltpu.VMEM
    tall = (5, planes + 3, span, lanes)
    rim = (planes + 2, span, lanes)
    outs = pl.pallas_call(
        functools.partial(kernel, count, cells),
        out_shape=(
            jax.ShapeDtypeStruct(state.shape, F32),
            jax.ShapeDtypeStruct(weight_in.shape, F32),
            jax.ShapeDtypeStruct((1, hid), F32),
            jax.ShapeDtypeStruct(weight_mid.shape, F32),
            jax.ShapeDtypeStruct((1, hid), F32),
            jax.ShapeDtypeStruct((weight_out.shape[1], hid), F32),
        ),
        in_specs=[pl.BlockSpec(memory_space=pltpu.VMEM)] * 10,
        out_specs=[pl.BlockSpec(memory_space=pltpu.VMEM)] * 6,
        scratch_shapes=[
            vmem(tall, F32),
            vmem(tall, F32),
            vmem(tall, F32),
            vmem(tall, F32),
            vmem((3,) + rim, F32),
            vmem((2, 3) + rim, F32),
            vmem((2, 3, 1, span, lanes), F32),
            vmem((2, 2, 3, 1, span, lanes), F32),
            vmem((2, rows * 16, lanes), F32),
            vmem((rows * 8, lanes), F32),
            vmem((rows * 8, lanes), F32),
            vmem((rows * 16, lanes), F32),
            vmem((chunks, hid, wide), F32),
            vmem((chunks, hid, wide), F32),
            vmem((hid, hid), BF16),
            vmem((2 * hid, 2 * hid), BF16),
            vmem((hid, hid), BF16),
            vmem((32, 2 * hid), BF16),
            vmem((2 * hid, 2 * hid), BF16),
            vmem((32, 2 * hid), BF16),
            vmem((hid, lanes), F32),
            vmem((2 * hid + 16, 2 * hid), F32),
            vmem((48, 2 * hid), F32),
            vmem((32, 2 * hid), F32),
            vmem((2, GROUP, 1, lanes), F32),
            vmem((2, far, 1, lanes), F32),
            vmem((GROUP, 16, lanes), F32),
            vmem((GROUP, 16, lanes), F32),
            vmem((GROUP, 16, lanes), F32),
            vmem((far, 16, lanes), F32),
            dma((7, 2)),
            dma((7, 2)),
            dma((2, GROUP)),
            dma((2, GROUP)),
            dma((GROUP,)),
            dma((GROUP,)),
            dma((GROUP,)),
            dma((GROUP,)),
            dma((3, far)),
            dma((3, far)),
        ],
        compiler_params=pltpu.CompilerParams(
            collective_id=0, has_side_effects=True, vmem_limit_bytes=48 * 1024 * 1024
        ),
        cost_estimate=pl.CostEstimate(
            flops=6 * 2 * 2 * 20000 * rows * lanes, bytes_accessed=2000000, transcendentals=0
        ),
    )(
        state,
        cotangent,
        weight_in,
        bias_in[None],
        weight_mid,
        bias_mid[None],
        weight_out.T,
        cell_index,
        segment_id,
        segment_coef[None],
    )
    return outs[0], outs[1], outs[2][0], outs[3], outs[4][0], outs[5].T


def solution(mesh):
    return jax.shard_map(
        shards,
        mesh=mesh,
        in_specs=(
            P(None, ("grp", "gx"), None, None),
            P(None, ("grp", "gx"), None, None),
            P(),
            P(),
            P(),
            P(),
            P(),
            P(None, "grp"),
            P(None, "grp"),
            P(),
        ),
        out_specs=(
            P(None, ("grp", "gx"), None, None),
            P("grp", None),
            P("grp"),
            P("grp", None),
            P("grp"),
            P("grp", None),
        ),
        check_vma=False,
    )
```

```python
import functools
import math

import jax
import jax.numpy as jnp
from jax import lax
from jax.experimental import pallas as pl
from jax.experimental.pallas import tpu as pltpu
from jax.sharding import PartitionSpec as P

MEAN_WIND = 0.5
TIME_STEP = 0.2
CLOSURE_SCALE = 0.1
EPSILON = 1e-05
F32 = jnp.float32
BF16 = jnp.bfloat16
ROWS = 16
GROUP = 16
MESH = pl.DeviceIdType.MESH


def split(value):
    high = value.astype(BF16)
    return high, (value - high.astype(F32)).astype(BF16)


def dot(left, right):
    return jnp.dot(left, right, preferred_element_type=F32)


def dot_nt(left, right):
    return lax.dot_general(left, right, (((1,), (1,)), ((), ())), preferred_element_type=F32)


def along_y(field):
    return (pltpu.roll(field, field.shape[1] - 1, 1) - pltpu.roll(field, 1, 1)) * 0.5


def along_z(field):
    return (pltpu.roll(field, field.shape[2] - 1, 2) - pltpu.roll(field, 1, 2)) * 0.5


def kernel(
    count,
    cells,
    state,
    cotangent,
    weight_in,
    bias_in,
    weight_mid,
    bias_mid,
    weight_out,
    cell_index,
    segment_id,
    segment_coef,
    grad_state,
    grad_in,
    grad_bias_in,
    grad_mid,
    grad_bias_mid,
    grad_out,
    pad_state,
    pad_middle,
    pad_cot,
    pad_carry,
    pad_stress,
    pad_grad,
    send_mid,
    recv_mid,
    send_grad,
    send_high,
    send_low,
    recv_low,
    recv_high,
    feats,
    stress,
    dstress,
    dfeats,
    hidden_one,
    hidden_two,
    left_one,
    left_mid,
    left_stress,
    left_out,
    left_back,
    left_feat,
    bias_two,
    acc_mid,
    acc_in,
    acc_out,
    sum_slots,
    sum_far,
    grad_parts,
    grad_slots,
    grad_total,
    grad_far,
    halo_send,
    halo_recv,
    sum_send,
    sum_recv,
    red_send,
    red_recv,
    gat_send,
    gat_recv,
    far_send,
    far_recv,
):
    planes = state.shape[1]
    span = state.shape[2]
    lanes = state.shape[3]
    rows = planes * span
    wide = ROWS * lanes
    per_plane = span // ROWS
    hid = weight_mid.shape[0]
    far = count // GROUP
    me = lax.axis_index("gx")
    mine = lax.rem(me, GROUP)
    base = me - mine
    block = me // GROUP
    right = lax.rem(me + 1, count)
    left = lax.rem(me + count - 1, count)

    def mate(step):
        return lax.rem(mine + step, GROUP)

    def far_mate(step):
        return lax.rem(block + step, far)

    barrier = pltpu.get_barrier_semaphore()
    for peer in (left, right):
        pl.semaphore_signal(barrier, inc=1, device_id={"gx": peer}, device_id_type=MESH)
    for step in range(1, GROUP):
        pl.semaphore_signal(barrier, inc=1, device_id={"gx": base + mate(step)}, device_id_type=MESH)
    for step in range(1, far):
        pl.semaphore_signal(
            barrier, inc=1, device_id={"gx": far_mate(step) * GROUP + mine}, device_id_type=MESH
        )
    pl.semaphore_wait(barrier, 2 + GROUP - 1 + far - 1)

    def remote(source, target, send, recv, peer):
        copy = pltpu.make_async_remote_copy(
            src_ref=source,
            dst_ref=target,
            send_sem=send,
            recv_sem=recv,
            device_id={"gx": peer},
            device_id_type=MESH,
        )
        copy.start()
        return copy

    def exchange(slot, to_right, at_low, to_left, at_high):
        return (
            remote(to_right, at_low, halo_send.at[slot, 0], halo_recv.at[slot, 0], right),
            remote(to_left, at_high, halo_send.at[slot, 1], halo_recv.at[slot, 1], left),
        )

    def finish(copies):
        for copy in copies:
            copy.wait()

    def halo(slot, source, start, target, low, high):
        return exchange(
            slot,
            source.at[:, start + planes - low : start + planes],
            target.at[:, 0:low],
            source.at[:, start : start + high],
            target.at[:, low + planes : low + planes + high],
        )

    state_copies = halo(0, state, 0, pad_state, 2, 1)
    cot_copies = halo(1, cotangent, 0, pad_cot, 1, 2)
    pad_state[:, 2 : 2 + planes] = state[...]
    pad_cot[:, 1 : 1 + planes] = cotangent[...]

    zeros_tail = jnp.zeros((8, lanes), F32)
    pack = jnp.concatenate(
        [weight_in[...], bias_in[...], bias_mid[...], weight_out[...], zeros_tail], axis=0
    )
    pack_high, pack_low = split(pack)
    high = pack_high.astype(F32)
    low = pack_low.astype(F32)

    def turned(parts):
        used = sum(part.shape[0] for part in parts)
        return jnp.concatenate(parts + [jnp.zeros((hid - used, lanes), F32)], axis=0).T.astype(BF16)

    left_one[...] = turned([high[:16], high[:16], low[:16], high[16:], low[16:]])
    left_stress[...] = turned([high[16:], high[16:], low[16:]])

    def stacked(value_high, value_low):
        return jnp.concatenate(
            [
                jnp.concatenate([value_high, value_high], axis=1),
                jnp.concatenate([value_low, value_low], axis=1),
            ],
            axis=0,
        )

    left_mid[...] = stacked(*split(weight_mid[...].T))
    left_back[...] = stacked(*split(weight_mid[...]))
    left_out[...] = stacked(pack_high[16:], pack_low[16:])
    left_feat[...] = stacked(pack_high[:16], pack_low[:16])
    turned_bias = jnp.concatenate([bias_mid[...], jnp.zeros((hid - 1, lanes), F32)], axis=0).T
    bias_two[...] = jnp.broadcast_to(turned_bias[:, 0:1], (hid, lanes))
    first_row = lax.broadcasted_iota(jnp.int32, (16, wide), 0) == 0
    ones_row = jnp.where(first_row, 1.0, 0.0).astype(BF16)

    def cell_coefficient(slot):
        index = cell_index[slot : slot + 1, :]
        points = index.shape[1]
        segments = segment_coef.shape[1]
        chosen = (
            lax.broadcasted_iota(jnp.int32, (segments, points), 0) == segment_id[slot : slot + 1, :]
        )
        picked = jnp.where(chosen, 1.0, 0.0)
        coef = lax.dot(
            jnp.broadcast_to(segment_coef[...], (8, segments)),
            picked,
            precision=lax.Precision.HIGHEST,
            preferred_element_type=F32,
        )[0:1]
        row = lax.div(index, jnp.int32(lanes)) - me * rows
        lane = lax.rem(index, jnp.int32(lanes))
        at_row = jnp.where(lax.broadcasted_iota(jnp.int32, (rows, points), 0) == row, 1.0, 0.0)
        at_lane = jnp.where(lax.broadcasted_iota(jnp.int32, (lanes, points), 0) == lane, coef, 0.0)
        return lax.dot_general(
            at_row,
            at_lane,
            (((1,), (1,)), ((), ())),
            precision=lax.Precision.HIGHEST,
            preferred_element_type=F32,
        ).reshape(planes, span, lanes)

    coef_zero = cell_coefficient(0)
    coef_one = cell_coefficient(1)
    acc_mid[...] = jnp.zeros_like(acc_mid)
    acc_in[...] = jnp.zeros_like(acc_in)
    acc_out[...] = jnp.zeros_like(acc_out)
    dstress[...] = jnp.zeros_like(dstress)

    def shifted(ref, comp, low, shift):
        return ref[comp, low + shift : low + shift + planes]

    def along_x(ref, comp, low):
        return (shifted(ref, comp, low, 1) - shifted(ref, comp, low, -1)) * 0.5

    def gradients(ref):
        table = []
        for comp in (1, 2, 3):
            centre = shifted(ref, comp, 2, 0)
            table.append([along_x(ref, comp, 2), along_y(centre), along_z(centre)])
        return table

    def scale_start(slot, table):
        total = None
        for line in table:
            for entry in line:
                total = entry * entry if total is None else total + entry * entry
        total = jnp.sum(total, axis=0)
        total = jnp.sum(total, axis=0, keepdims=True)
        sum_slots[slot, mine] = total
        return [
            remote(
                sum_slots.at[slot, mine],
                sum_slots.at[slot, mine],
                sum_send.at[slot, step],
                sum_recv.at[slot, step],
                base + mate(step),
            )
            for step in range(1, GROUP)
        ]

    def wait_sums(slot, copies):
        for step, copy in zip(range(1, GROUP), copies):
            copy.wait_send()
            source = mate(GROUP - step)
            pltpu.make_async_remote_copy(
                src_ref=sum_slots.at[slot, source],
                dst_ref=sum_slots.at[slot, source],
                send_sem=sum_send.at[slot, step],
                recv_sem=sum_recv.at[slot, step],
                device_id={"gx": base + mate(step)},
                device_id_type=MESH,
            ).wait_recv()

    def scale_finish(slot, copies):
        wait_sums(slot, copies)
        total = jnp.sum(sum_slots[slot], axis=0)
        if far > 1:
            sum_far[slot, 0] = total
            others = [
                remote(
                    sum_far.at[slot, 0],
                    sum_far.at[slot, step],
                    far_send.at[slot, step],
                    far_recv.at[slot, step],
                    far_mate(step) * GROUP + mine,
                )
                for step in range(1, far)
            ]
            finish(others)
            total = jnp.sum(sum_far[slot], axis=0)
        total = jnp.sum(total, axis=1, keepdims=True)
        return lax.rsqrt(total / cells + EPSILON).reshape(1, 1, 1)

    def put(ref, slot, width, value):
        ref[pl.ds(slot, rows, stride=width), :] = value.reshape(rows, lanes)

    def get(ref, slot, width, plane=0, number=planes):
        start = plane * span * width + slot
        return ref[pl.ds(start, number * span, stride=width), :].reshape(number, span, lanes)

    def write_features(section, ref, table, inverse):
        target = feats.at[section]
        scaled = [[entry * inverse for entry in line] for line in table]
        sym = None
        skew = None
        for a in range(3):
            for b in range(3):
                put(target, 3 * a + b, 16, scaled[a][b])
                plus = 0.5 * (scaled[a][b] + scaled[b][a])
                minus = 0.5 * (scaled[a][b] - scaled[b][a])
                sym = plus * plus if sym is None else sym + plus * plus
                if a != b:
                    skew = minus * minus if skew is None else skew + minus * minus
        for slot, comp in enumerate((1, 2, 3, 0, 4)):
            put(target, 9 + slot, 16, shifted(ref, comp, 2, 0))
        put(target, 14, 16, sym)
        put(target, 15, 16, skew)

    def columns(ref, chunk, height):
        start = chunk * (ROWS * height)
        return jnp.concatenate(
            [
                ref[pl.ds(pl.multiple_of(start + row * height, 8), height), :]
                for row in range(ROWS)
            ],
            axis=1,
        )

    def spread(ref, chunk, height, value):
        start = chunk * (ROWS * height)
        for row in range(ROWS):
            ref[pl.ds(pl.multiple_of(start + row * height, 8), height), :] = value[
                :height, row * lanes : (row + 1) * lanes
            ]

    def halves(value):
        size = value.shape[0] // 2
        return value[:size] + value[size:]

    def forward(section, chunk):
        feat_high, feat_low = split(columns(feats.at[section], chunk, 16))
        blank = jnp.zeros((hid - 80, wide), BF16)
        one = jnp.tanh(
            dot(
                left_one[...],
                jnp.concatenate([feat_high, feat_low, feat_high, ones_row, ones_row, blank], axis=0),
            )
        )
        one_parts = jnp.concatenate(split(one), axis=0)
        bias = jnp.concatenate([bias_two[...]] * ROWS, axis=1)
        two = jnp.tanh(halves(dot(left_mid[...], one_parts)) + bias)
        two_parts = jnp.concatenate(split(two), axis=0)
        return (feat_high, feat_low), one, one_parts, two, two_parts

    def backward(chunk, feat, one, one_parts, two, two_parts):
        small = jnp.concatenate([columns(dstress, chunk, 8), jnp.zeros((8, wide), F32)], axis=0)
        small_high, small_low = split(small)
        blank = jnp.zeros((hid - 48, wide), BF16)
        back_two = dot(
            left_stress[...],
            jnp.concatenate([small_high, small_low, small_high, blank], axis=0),
        )
        pre_two = jnp.concatenate(split(back_two * (1.0 - two * two)), axis=0)
        back_one = halves(dot(left_back[...], pre_two))
        pre_one = jnp.concatenate(split(back_one * (1.0 - one * one)), axis=0)
        spread(dfeats, chunk, 16, halves(dot(left_feat[...], pre_one)))
        acc_mid[...] += dot_nt(jnp.concatenate([one_parts, ones_row], axis=0), pre_two)
        acc_in[...] += dot_nt(jnp.concatenate([feat[0], feat[1], ones_row], axis=0), pre_one)
        acc_out[...] += dot_nt(jnp.concatenate([small_high, small_low], axis=0), two_parts)

    def forward_zero(chunk):
        _, one, _, two, two_parts = forward(0, chunk)
        hidden_one[chunk] = one
        hidden_two[chunk] = two
        spread(stress, chunk, 8, halves(dot(left_out[...], two_parts)))

    def both_one(chunk):
        backward(chunk, *forward(1, chunk))

    def backward_zero(chunk):
        one = hidden_one[chunk]
        two = hidden_two[chunk]
        feat = split(columns(feats.at[0], chunk, 16))
        one_parts = jnp.concatenate(split(one), axis=0)
        two_parts = jnp.concatenate(split(two), axis=0)
        backward(chunk, feat, one, one_parts, two, two_parts)

    def sweep(body, between, first, last):
        first, last = first * per_plane, last * per_plane
        chunks = planes * per_plane

        def outer(step, carry):
            body(jnp.where(step < first, step, step + (chunks - first - last)))
            return carry

        def inner(step, carry):
            body(step)
            return carry

        lax.fori_loop(0, first + last, outer, 0)
        between()
        lax.fori_loop(first, chunks - last, inner, 0)

    def upwind(ref, comp):
        return (
            2.0 * shifted(ref, comp, 2, 1)
            + 3.0 * shifted(ref, comp, 2, 0)
            - 6.0 * shifted(ref, comp, 2, -1)
            + shifted(ref, comp, 2, -2)
        ) * (-MEAN_WIND / 6.0)

    def upwind_back(ref, comp):
        return (
            2.0 * shifted(ref, comp, 1, -1)
            + 3.0 * shifted(ref, comp, 1, 0)
            - 6.0 * shifted(ref, comp, 1, 1)
            + shifted(ref, comp, 1, 2)
        ) * (-MEAN_WIND / 6.0)

    def write_dstress(ref, factor):
        factor = -factor * CLOSURE_SCALE
        u, v, w = (shifted(ref, comp, 1, 0) for comp in (1, 2, 3))
        put(dstress, 2, 8, along_x(ref, 1, 1) * factor)
        put(dstress, 3, 8, along_y(v) * factor)
        put(dstress, 4, 8, along_z(w) * factor)
        put(dstress, 5, 8, (along_y(u) + along_x(ref, 2, 1)) * factor)
        put(dstress, 6, 8, (along_z(u) + along_x(ref, 3, 1)) * factor)
        put(dstress, 7, 8, (along_z(v) + along_y(w)) * factor)

    def dgradient(section, a, b, inverse, plane, number):
        ref = feats.at[section]
        total = get(dfeats, 3 * a + b, 16, plane, number)
        sym = get(dfeats, 14, 16, plane, number)
        here = get(ref, 3 * a + b, 16, plane, number)
        there = get(ref, 3 * b + a, 16, plane, number)
        total = total + (here + there) * sym
        if a != b:
            total = total + (here - there) * get(dfeats, 15, 16, plane, number)
        return total * inverse

    def send_dgradient():
        for a in range(3):
            send_grad[0, a] = dgradient(0, a, 0, inverse_zero, planes - 1, 1)
            send_grad[1, a] = dgradient(0, a, 0, inverse_zero, 0, 1)
        return exchange(
            6,
            send_grad.at[0],
            pad_grad.at[0, :, 0:1],
            send_grad.at[1],
            pad_grad.at[0, :, planes + 1 : planes + 2],
        )

    def send_carry():
        top = closure_local(1, inverse_one, linear, planes - 1, 1)
        low = closure_local(1, inverse_one, linear, 0, 2)
        for a in range(3):
            start = dgradient(1, a, 0, inverse_one, 0, 3)
            end = dgradient(1, a, 0, inverse_one, planes - 2, 2)
            send_high[a] = end[1]
            send_low[a] = start[0]
            top[1 + a] = top[1 + a] + 0.5 * end[0:1]
            send_low[3 + 2 * (1 + a)] = low[1 + a][0] - 0.5 * start[1]
            send_low[4 + 2 * (1 + a)] = low[1 + a][1] - 0.5 * (start[2] - start[0])
        for comp in range(5):
            send_high[3 + comp] = top[comp][0]
        for comp in (0, 4):
            send_low[3 + 2 * comp] = low[comp][0]
            send_low[4 + 2 * comp] = low[comp][1]
        return exchange(5, send_high, recv_low, send_low, recv_high)

    def back_linear(ref, factor, speed_ref, coef):
        mass_rho = shifted(ref, 0, 1, 0) + shifted(ref, 4, 1, 0)
        mass_x = along_x(ref, 0, 1) + along_x(ref, 4, 1)
        u, v, w = (shifted(ref, comp, 1, 0) for comp in (1, 2, 3))
        speed = MEAN_WIND + shifted(speed_ref, 1, 2, 0)
        return [
            upwind_back(ref, 0) * factor,
            (upwind_back(ref, 1) + mass_x - 2.0 * coef * jnp.abs(speed) * u) * factor,
            (upwind_back(ref, 2) + along_y(mass_rho)) * factor,
            (upwind_back(ref, 3) + along_z(mass_rho)) * factor,
            (upwind_back(ref, 4) + along_x(ref, 1, 1) + along_y(v) + along_z(w)) * factor,
        ]

    def closure_local(section, inverse, linear, plane, number):
        total = [entry[plane : plane + number] for entry in linear]
        for slot, comp in enumerate((1, 2, 3, 0, 4)):
            total[comp] = total[comp] + get(dfeats, 9 + slot, 16, plane, number)
        for a in range(3):
            total[1 + a] = (
                total[1 + a]
                - along_y(dgradient(section, a, 1, inverse, plane, number))
                - along_z(dgradient(section, a, 2, inverse, plane, number))
            )
        return total

    def back_closure(section, inverse, linear, arrive):
        for a in range(3):
            pad_grad[section, a, 1 : 1 + planes] = dgradient(section, a, 0, inverse, 0, planes)
        total = closure_local(section, inverse, linear, 0, planes)
        arrive()
        ref = pad_grad.at[section]
        for a in range(3):
            total[1 + a] = total[1 + a] - along_x(ref, a, 1)
        return total

    finish(state_copies)
    table = gradients(pad_state)
    copies = scale_start(0, table)
    divergence = table[0][0] + table[1][1] + table[2][2]
    speed = MEAN_WIND + shifted(pad_state, 1, 2, 0)
    pressure = shifted(pad_state, 4, 2, 0)
    rate = [
        upwind(pad_state, 0) - divergence,
        upwind(pad_state, 1) - along_x(pad_state, 4, 2) - coef_zero * speed * jnp.abs(speed),
        upwind(pad_state, 2) - along_y(pressure),
        upwind(pad_state, 3) - along_z(pressure),
        upwind(pad_state, 4) - divergence,
    ]
    for comp in range(5):
        pad_middle[comp, 2 : 2 + planes] = (
            shifted(pad_state, comp, 2, 0) + TIME_STEP * rate[comp]
        )
    finish(cot_copies)
    write_dstress(pad_cot, 0.25 * TIME_STEP)
    inverse_zero = scale_finish(0, copies)
    write_features(0, pad_state, table, inverse_zero)
    stress_copies = []
    gain = TIME_STEP * CLOSURE_SCALE

    def stress_terms(plane, number):
        s_yy, s_zz, s_xy, s_xz, s_yz = (
            get(stress, 2 + entry, 8, plane, number) for entry in (1, 2, 3, 4, 5)
        )
        return (
            along_y(s_xy) + along_z(s_xz),
            along_y(s_yy) + along_z(s_yz),
            along_y(s_yz) + along_z(s_zz),
        )

    def send_edges():
        top = stress_terms(planes - 1, 1)
        low = stress_terms(0, 1)
        for slot, entry in enumerate((0, 3, 4)):
            end = get(stress, 2 + entry, 8, planes - 2, 2)
            start = get(stress, 2 + entry, 8, 0, 2)
            send_mid[0, slot] = end[1]
            send_mid[1, slot] = start[0]
            send_mid[0, 3 + slot] = pad_middle[1 + slot, 1 + planes] + gain * (
                top[slot][0] - 0.5 * end[0]
            )
            send_mid[1, 3 + slot] = pad_middle[1 + slot, 2] + gain * (low[slot][0] + 0.5 * start[1])
        stress_copies.extend(
            exchange(2, send_mid.at[0], recv_mid.at[0], send_mid.at[1], recv_mid.at[1])
        )

    sweep(forward_zero, send_edges, 2, 2)
    for slot, entry in enumerate((0, 3, 4)):
        pad_stress[slot, 1 : 1 + planes] = get(stress, 2 + entry, 8)
    subs = stress_terms(0, planes)
    finish(stress_copies)
    for slot in range(3):
        pad_stress[slot, 0] = recv_mid[0, slot]
        pad_stress[slot, planes + 1] = recv_mid[1, slot]
        here = shifted(pad_middle, 1 + slot, 2, 0)
        pad_middle[1 + slot, 2 : 2 + planes] = here + gain * (
            subs[slot] + along_x(pad_stress, slot, 1)
        )
        pad_middle[1 + slot, 1] = recv_mid[0, 3 + slot] + 0.5 * gain * pad_stress[slot, 1]
        pad_middle[1 + slot, 2 + planes] = (
            recv_mid[1, 3 + slot] - 0.5 * gain * pad_stress[slot, planes]
        )

    table = gradients(pad_middle)
    copies = scale_start(1, table)
    linear = back_linear(pad_cot, 0.25 * TIME_STEP, pad_middle, coef_one)
    for comp in range(5):
        linear[comp] = linear[comp] + 0.25 * cotangent[comp]
    inverse_one = scale_finish(1, copies)
    write_features(1, pad_middle, table, inverse_one)
    grad_copies = []
    carry_copies = []
    sweep(both_one, lambda: carry_copies.extend(send_carry()), 3, 2)

    def carry_arrives():
        finish(carry_copies)
        for a in range(3):
            pad_grad[1, a, 0] = recv_low[a]
            pad_grad[1, a, planes + 1] = recv_high[a]

    carried = back_closure(1, inverse_one, linear, carry_arrives)
    for comp in range(5):
        pad_carry[comp, 1 : 1 + planes] = carried[comp]
        low = recv_low[3 + comp]
        top = recv_high[3 + 2 * comp]
        if 1 <= comp <= 3:
            low = low - 0.5 * pad_grad[1, comp - 1, 1]
            top = top + 0.5 * pad_grad[1, comp - 1, planes]
        pad_carry[comp, 0] = low
        pad_carry[comp, 1 + planes] = top
        pad_carry[comp, 2 + planes] = recv_high[4 + 2 * comp]

    write_dstress(pad_carry, TIME_STEP)
    linear = back_linear(pad_carry, TIME_STEP, pad_state, coef_zero)
    for comp in range(5):
        linear[comp] = linear[comp] + (0.75 * cotangent[comp] + shifted(pad_carry, comp, 1, 0))
    grad_copies = []
    sweep(backward_zero, lambda: grad_copies.extend(send_dgradient()), 1, 1)

    factor = 1.0 / (TIME_STEP * CLOSURE_SCALE * math.sqrt(cells))

    def folded(value):
        return (value[:, :hid] + value[:, hid:]) * factor

    both = folded(acc_mid[...])
    mid = both[:hid] + both[hid : 2 * hid]
    narrow = folded(acc_in[...])
    out = folded(acc_out[...])
    rest = jnp.concatenate(
        [
            narrow[:16] + narrow[16:32],
            narrow[32:33],
            both[2 * hid : 2 * hid + 1],
            (out[:16] + out[16:])[2:8],
        ],
        axis=0,
    )
    for slot in range(GROUP):
        grad_parts[slot, 0:8] = mid[8 * slot : 8 * slot + 8]
        if slot < 3:
            grad_parts[slot, 8:16] = rest[8 * slot : 8 * slot + 8]
        else:
            grad_parts[slot, 8:16] = jnp.zeros((8, lanes), F32)
    reduce_copies = [
        remote(
            grad_parts.at[mate(step)],
            grad_slots.at[step],
            red_send.at[step],
            red_recv.at[step],
            base + mate(step),
        )
        for step in range(1, GROUP)
    ]
    result = back_closure(0, inverse_zero, linear, lambda: finish(grad_copies))
    for comp in range(5):
        grad_state[comp] = result[comp]
    grad_slots[0] = grad_parts[mine]
    finish(reduce_copies)
    owned = jnp.sum(grad_slots[...], axis=0)
    if far > 1:
        grad_far[0] = owned
        others = [
            remote(
                grad_far.at[0],
                grad_far.at[step],
                far_send.at[2, step],
                far_recv.at[2, step],
                far_mate(step) * GROUP + mine,
            )
            for step in range(1, far)
        ]
        finish(others)
        owned = jnp.sum(grad_far[...], axis=0)
    grad_total[mine] = owned
    gather_copies = [
        remote(
            grad_total.at[mine],
            grad_total.at[mine],
            gat_send.at[step],
            gat_recv.at[step],
            base + mate(step),
        )
        for step in range(1, GROUP)
    ]
    for step, copy in zip(range(1, GROUP), gather_copies):
        copy.wait_send()
        source = mate(GROUP - step)
        pltpu.make_async_remote_copy(
            src_ref=grad_total.at[source],
            dst_ref=grad_total.at[source],
            send_sem=gat_send.at[step],
            recv_sem=gat_recv.at[step],
            device_id={"gx": base + mate(step)},
            device_id_type=MESH,
        ).wait_recv()
    for slot in range(GROUP):
        grad_mid[8 * slot : 8 * slot + 8, :] = grad_total[slot, 0:8]
    grad_in[0:8, :] = grad_total[0, 8:16]
    grad_in[8:16, :] = grad_total[1, 8:16]
    grad_bias_in[...] = grad_total[2, 8:9]
    grad_bias_mid[...] = grad_total[2, 9:10]
    grad_out[...] = grad_total[2, 10:16]


def shards(
    state,
    cotangent,
    weight_in,
    bias_in,
    weight_mid,
    bias_mid,
    weight_out,
    cell_index,
    segment_id,
    segment_coef,
):
    count = lax.axis_size("gx")
    planes, span, lanes = state.shape[1:]
    cells = count * planes * span * lanes
    rows = planes * span
    chunks = rows // ROWS
    wide = ROWS * lanes
    hid = weight_mid.shape[0]
    far = count // GROUP
    dma = pltpu.SemaphoreType.DMA
    vmem = pltpu.VMEM
    tall = (5, planes + 3, span, lanes)
    rim = (planes + 2, span, lanes)
    outs = pl.pallas_call(
        functools.partial(kernel, count, cells),
        out_shape=(
            jax.ShapeDtypeStruct(state.shape, F32),
            jax.ShapeDtypeStruct(weight_in.shape, F32),
            jax.ShapeDtypeStruct((1, hid), F32),
            jax.ShapeDtypeStruct(weight_mid.shape, F32),
            jax.ShapeDtypeStruct((1, hid), F32),
            jax.ShapeDtypeStruct((weight_out.shape[1], hid), F32),
        ),
        in_specs=[pl.BlockSpec(memory_space=pltpu.VMEM)] * 10,
        out_specs=[pl.BlockSpec(memory_space=pltpu.VMEM)] * 6,
        scratch_shapes=[
            vmem(tall, F32),
            vmem(tall, F32),
            vmem(tall, F32),
            vmem(tall, F32),
            vmem((3,) + rim, F32),
            vmem((2, 3) + rim, F32),
            vmem((2, 6, span, lanes), F32),
            vmem((2, 6, span, lanes), F32),
            vmem((2, 3, 1, span, lanes), F32),
            vmem((8, span, lanes), F32),
            vmem((13, span, lanes), F32),
            vmem((8, span, lanes), F32),
            vmem((13, span, lanes), F32),
            vmem((2, rows * 16, lanes), F32),
            vmem((rows * 8, lanes), F32),
            vmem((rows * 8, lanes), F32),
            vmem((rows * 16, lanes), F32),
            vmem((chunks, hid, wide), F32),
            vmem((chunks, hid, wide), F32),
            vmem((hid, hid), BF16),
            vmem((2 * hid, 2 * hid), BF16),
            vmem((hid, hid), BF16),
            vmem((32, 2 * hid), BF16),
            vmem((2 * hid, 2 * hid), BF16),
            vmem((32, 2 * hid), BF16),
            vmem((hid, lanes), F32),
            vmem((2 * hid + 16, 2 * hid), F32),
            vmem((48, 2 * hid), F32),
            vmem((32, 2 * hid), F32),
            vmem((2, GROUP, 1, lanes), F32),
            vmem((2, far, 1, lanes), F32),
            vmem((GROUP, 16, lanes), F32),
            vmem((GROUP, 16, lanes), F32),
            vmem((GROUP, 16, lanes), F32),
            vmem((far, 16, lanes), F32),
            dma((7, 2)),
            dma((7, 2)),
            dma((2, GROUP)),
            dma((2, GROUP)),
            dma((GROUP,)),
            dma((GROUP,)),
            dma((GROUP,)),
            dma((GROUP,)),
            dma((3, far)),
            dma((3, far)),
        ],
        compiler_params=pltpu.CompilerParams(
            collective_id=0, has_side_effects=True, vmem_limit_bytes=48 * 1024 * 1024
        ),
        cost_estimate=pl.CostEstimate(
            flops=6 * 2 * 2 * 20000 * rows * lanes, bytes_accessed=2000000, transcendentals=0
        ),
    )(
        state,
        cotangent,
        weight_in,
        bias_in[None],
        weight_mid,
        bias_mid[None],
        weight_out.T,
        cell_index,
        segment_id,
        segment_coef[None],
    )
    return outs[0], outs[1], outs[2][0], outs[3], outs[4][0], outs[5].T


def solution(mesh):
    return jax.shard_map(
        shards,
        mesh=mesh,
        in_specs=(
            P(None, ("grp", "gx"), None, None),
            P(None, ("grp", "gx"), None, None),
            P(),
            P(),
            P(),
            P(),
            P(),
            P(None, "grp"),
            P(None, "grp"),
            P(),
        ),
        out_specs=(
            P(None, ("grp", "gx"), None, None),
            P("grp", None),
            P("grp"),
            P("grp", None),
            P("grp"),
            P("grp", None),
        ),
        check_vma=False,
    )
```
